128 devices in a mesh: fsdp: 16 (over y, z), tp: 8 (over x, core).
Axes of the slice: x: 4, y: 4, z: 4, core: 2. Of those that a mesh axis runs over, the one named last changes fastest.
Arguments:
- tokens: bfloat16 [4096, 4096], P('fsdp', 'tp'), may hold values from -6 to 6
- gate_tiles: bfloat16 [288, 1024, 128], P('fsdp', 'tp'), may hold values from -0.125 to 0.125
- up_tiles: bfloat16 [288, 1024, 128], P('fsdp', 'tp'), may hold values from -0.125 to 0.125
- gate_slots: int32 [288, 8], P(None, 'tp'), may hold values from -1 to 27, as said below
- up_slots: int32 [288, 8], P(None, 'tp'), may hold values from -1 to 27, as said below
- cotangent: bfloat16 [4096, 14336], P('fsdp', 'tp'), may hold values from -6 to 6
Outputs:
- hidden: bfloat16 [4096, 14336], P('fsdp', 'tp')
- input_grad: bfloat16 [4096, 4096], P('fsdp', 'tp')
- gate_tile_grad: bfloat16 [288, 1024, 128], P('fsdp', 'tp')
- up_tile_grad: bfloat16 [288, 1024, 128], P('fsdp', 'tp')
The draws below stay inside these ranges and needn't reach their ends.
Inputs may be any that keep to these rules, and one draw needn't show every extreme that they name: `gate_slots`: for each owner (rows f * 18 to (f + 1) * 18 - 1, column t) the non-negative entries are distinct positions of that owner, stand before its -1 entries, and number 10 to 18; in every draw some owner fills all 18 slots. `up_slots`: as for gate_slots, drawn independently.
All inputs are finite; a program needn't handle non-finite values.
Results may differ from the reference program's by a relative error of at most 0.02.
Values may be sent and summed in bfloat16 or wider, within the bound.
No kernel may reach another device: no remote copies, remote signals or barrier semaphores. Data moves between devices by JAX's collectives and lax.ppermute only.
A program may use at most 192 MiB of HBM per device.

```python
import jax
import jax.numpy as jnp
from jax import lax

D = 4096
FF = 14336
TILE = 128
TOK_DEV = 256
TOKENS = 4096
OWNER_TILES = 28
CAP = 18
LOW = 10
N_FSDP = 16
N_TP = 8


def slot_table(key):
    owners = N_FSDP * N_TP
    key_count, key_busy, key_order = jax.random.split(key, 3)
    counts = jax.random.randint(key_count, (owners,), LOW, CAP + 1)
    busiest = jax.random.randint(key_busy, (), 0, owners)
    counts = jnp.where(jnp.arange(owners) == busiest, CAP, counts)
    orders = jax.vmap(lambda sub_key: jax.random.permutation(sub_key, OWNER_TILES))(jax.random.split(key_order, owners))
    chosen = orders[:, :CAP]
    slot_index = jnp.arange(CAP)
    filled = jnp.where(slot_index[None, :] < counts[:, None], chosen, -1)
    filled = filled.reshape(N_FSDP, N_TP, CAP).transpose(0, 2, 1)
    return filled.reshape(N_FSDP * CAP, N_TP).astype(jnp.int32)


def draw_gate_slots(key, part):
    return slot_table(jax.random.fold_in(key, 11))


def draw_up_slots(key, part):
    return slot_table(jax.random.fold_in(key, 23))


def block_scale(key, shape, cuts, smallest, largest):
    factor_of = 1.0
    for dim, parts in cuts:
        heights = jax.random.uniform(jax.random.fold_in(jax.random.fold_in(key, 6), dim), (parts,), jnp.float32, smallest / len(cuts), largest / len(cuts))
        factor_of = factor_of * jnp.repeat(jnp.exp(heights), shape[dim] // parts).reshape((-1,) + (1,) * (len(shape) - 1 - dim))
    return factor_of


def normal_values(stream_key, dims, scale, reach, cuts=(), kind=jnp.bfloat16):
    result = scale * jax.random.normal(stream_key, dims, jnp.float32)
    if cuts:
        result = result * block_scale(stream_key, dims, cuts, -0.22, 0.18)
    return jnp.clip(result, -reach, reach).astype(kind)


def setup_inputs(seed: int = 0) -> dict:
    key_of = jax.random.split(jax.random.key(seed), 7)
    tokens = normal_values(key_of[0], (TOKENS, D), 1.0, 6.0, ((0, 16), (1, 8)))
    gate_tiles = normal_values(key_of[1], (N_FSDP * CAP, N_TP * TILE, TILE), (D // 2) ** -0.5, 0.125, ((0, 16), (1, 8)))
    up_tiles = normal_values(key_of[2], (N_FSDP * CAP, N_TP * TILE, TILE), (D // 2) ** -0.5, 0.125, ((0, 16), (1, 8)))
    gate_slots = draw_gate_slots(jax.random.fold_in(key_of[6], 71), 0)
    up_slots = draw_up_slots(jax.random.fold_in(key_of[6], 71), 0)
    cotangent = normal_values(key_of[5], (TOKENS, FF), 1.0, 6.0, ((0, 16), (1, 8)))
    return dict(tokens=tokens, gate_tiles=gate_tiles, up_tiles=up_tiles, gate_slots=gate_slots, up_slots=up_slots, cotangent=cotangent)


def selector(slots):
    positions = jnp.arange(OWNER_TILES, dtype=jnp.int32)
    owned = slots.reshape(N_FSDP, CAP, N_TP).astype(jnp.int32)
    return (owned[..., None] == positions).astype(jnp.float32)


def unpack(tiles, slots):
    row_tiles = D // (TILE * N_FSDP)
    col_tiles = FF // (TILE * N_TP)
    blocks = tiles.astype(jnp.float32).reshape(N_FSDP, CAP, N_TP, TILE, TILE)
    dense_rows = jnp.einsum('fctp,fctab->ftpab', selector(slots), blocks)
    dense_rows = dense_rows.reshape(N_FSDP, N_TP, row_tiles, col_tiles, TILE, TILE)
    dense_rows = dense_rows.transpose(0, 2, 4, 1, 3, 5)
    return dense_rows.reshape(D, FF).astype(jnp.bfloat16)


def pack_tiles(summed, slots):
    row_tiles = D // (TILE * N_FSDP)
    col_tiles = FF // (TILE * N_TP)
    blocks = summed.reshape(N_FSDP, row_tiles, TILE, N_TP, col_tiles, TILE)
    blocks = blocks.transpose(0, 3, 1, 4, 2, 5).reshape(N_FSDP, N_TP, OWNER_TILES, TILE, TILE)
    packed = jnp.einsum('fctp,ftpab->fctab', selector(slots), blocks, precision=lax.Precision.HIGHEST)
    return packed.reshape(N_FSDP * CAP, N_TP * TILE, TILE).astype(jnp.bfloat16)


def reference(tokens, gate_tiles, up_tiles, gate_slots, up_slots, cotangent):
    w_gate = unpack(gate_tiles, gate_slots)
    w_up = unpack(up_tiles, up_slots)
    gate = jnp.dot(tokens, w_gate, preferred_element_type=jnp.float32)
    up = jnp.dot(tokens, w_up, preferred_element_type=jnp.float32)
    sigmoid_gate = jax.nn.sigmoid(gate)
    activated = gate * sigmoid_gate
    hidden = (activated * up).astype(jnp.bfloat16)
    upstream = cotangent.astype(jnp.float32)
    gate_grad = (upstream * up * sigmoid_gate * (1.0 + gate * (1.0 - sigmoid_gate))).astype(jnp.bfloat16)
    up_grad = (upstream * activated).astype(jnp.bfloat16)
    input_grad = (jnp.dot(gate_grad, w_gate.T, preferred_element_type=jnp.float32)
                  + jnp.dot(up_grad, w_up.T, preferred_element_type=jnp.float32)).astype(jnp.bfloat16)
    token_blocks = tokens.reshape(N_FSDP, TOK_DEV, D)
    gate_blocks = gate_grad.reshape(N_FSDP, TOK_DEV, FF)
    up_blocks = up_grad.reshape(N_FSDP, TOK_DEV, FF)

    def shard_step(totals, shard_item):
        token_rows, gate_rows, up_rows = shard_item
        partial_gate = jnp.dot(token_rows.T, gate_rows, preferred_element_type=jnp.float32)
        partial_up = jnp.dot(token_rows.T, up_rows, preferred_element_type=jnp.float32)
        partial_gate = lax.optimization_barrier(partial_gate.astype(jnp.bfloat16)).astype(jnp.float32)
        partial_up = lax.optimization_barrier(partial_up.astype(jnp.bfloat16)).astype(jnp.float32)
        return (totals[0] + partial_gate, totals[1] + partial_up), None

    zeros_start = jnp.zeros((D, FF), jnp.float32)
    (sum_gate, sum_up), _ = lax.scan(shard_step, (zeros_start, zeros_start), (token_blocks, gate_blocks, up_blocks))
    gate_tile_grad = pack_tiles(sum_gate, gate_slots)
    up_tile_grad = pack_tiles(sum_up, up_slots)
    return hidden, input_grad, gate_tile_grad, up_tile_grad
```

```python
import functools

import jax
import jax.numpy as jnp
from jax import lax
from jax.experimental import pallas as pl
from jax.experimental.pallas import tpu as pltpu
from jax.sharding import Mesh
from jax.sharding import PartitionSpec as P

RING = 4
TILE = 128
CAP = 18
HALF = CAP // 2
ROW_TILES = 2
COL_TILES = 14
TOK = 256
ROWS = ROW_TILES * TILE
FF = COL_TILES * TILE
ALL = RING * 256
STEP = 256
F32 = jnp.float32
BF16 = jnp.bfloat16
PARAMS = pltpu.CompilerParams(vmem_limit_bytes=40 * 2**20)


def shift(value, axis, by):
    return lax.ppermute(value, axis, [(i, (i + by) % RING) for i in range(RING)])


def gather_ring(value, axis):
    half = value.shape[0] // 2
    below = shift(value, axis, 1)
    above = shift(value, axis, -1)
    far_low = shift(below[:half], axis, 1)
    far_high = shift(above[half:], axis, -1)
    return value, below, above, far_low, far_high


def add(a, b):
    return (a.astype(F32) + b.astype(F32)).astype(BF16)


def scatter_ring(own, to_next, far_low, far_high, to_last, axis):
    half = far_low.shape[0]
    low = shift(far_low, axis, 1)
    high = shift(far_high, axis, -1)
    to_next = jnp.concatenate([add(to_next[:half], low), to_next[half:]], 0)
    to_last = jnp.concatenate([to_last[:half], add(to_last[half:], high)], 0)
    return own, shift(to_next, axis, 1), shift(to_last, axis, -1)


def swap_core(value):
    return lax.ppermute(value, "core", [(0, 1), (1, 0)])


def mod(value):
    return lax.rem(value + 2 * RING, RING)


def place_of(meta):
    return meta[0], meta[1], meta[2], meta[3]


def owner_base(kind, meta, distance):
    y, z, _, _ = place_of(meta)
    owner = mod(y + distance) * RING + z if kind == "gate" else y * RING + mod(z + distance)
    return owner * CAP


def fill_weights(kind, meta, slots, pieces, dense, position):
    dense[...] = jnp.zeros(dense.shape, dense.dtype)
    own, below, above, far_low, far_high = pieces
    for piece, distance, first, count in (
        (own, 0, 0, CAP),
        (below, 3, 0, CAP),
        (above, 1, 0, CAP),
        (far_low, 2, 0, HALF),
        (far_high, 2, HALF, HALF),
    ):
        base = owner_base(kind, meta, distance) + first
        row_base = position(distance) * ROWS

        def put(index, _, piece=piece, base=base, row_base=row_base):
            spot = slots[base + index]

            @pl.when(spot >= 0)
            def _():
                row = pl.multiple_of(row_base + lax.div(spot, COL_TILES) * TILE, TILE)
                col = pl.multiple_of(lax.rem(spot, COL_TILES) * TILE, TILE)
                dense[pl.ds(row, TILE), pl.ds(col, TILE)] = piece[index]

            return 0

        lax.fori_loop(0, count, put, 0)


def token_places(kind, meta):
    y, z, x, c = place_of(meta)
    places = []
    for core in (c, 1 - c):
        if kind == "gate":
            row = 2 * core * TOK
            for step, first, count in ((0, 0, 512), (-1, 0, 512), (1, 0, 512), (2, 0, 256), (2, 256, 256)):
                col = mod(x + step - y) * ROWS
                places.append(((0, count, 0, 256, row + first, col),))
        else:
            cols = [mod(2 * core + b - z) * ROWS for b in range(2)]
            for step, first, count in ((0, 0, 256), (-1, 0, 256), (1, 0, 256), (2, 0, 128), (2, 128, 128)):
                row = mod(x + step - y) * TOK + first
                places.append(tuple((0, count, 256 * b, 256, row, cols[b]) for b in range(2)))
    return places


def forward_kernel(kind, meta, slots, *refs):
    tokens, tiles = refs[:10], refs[10:15]
    own, to_next, far_low, far_high, to_last, together, dense = refs[15:]
    step = pl.program_id(0)

    @pl.when(step == 0)
    def _():
        fill_weights(kind, meta, slots, tiles, dense, lambda distance: distance)
        for ref, blocks in zip(tokens, token_places(kind, meta)):
            for row, rows, col, cols, to_row, to_col in blocks:
                together[
                    pl.ds(pl.multiple_of(to_row, TILE), rows),
                    pl.ds(pl.multiple_of(to_col, TILE), cols),
                ] = ref[row : row + rows, col : col + cols]

    weights = dense[:, pl.ds(pl.multiple_of(step * STEP, STEP), STEP)]
    share = jnp.dot(together[...], weights, preferred_element_type=F32).astype(BF16)
    own[...] = share[:TOK]
    to_next[...] = share[TOK : 2 * TOK]
    far_low[...] = share[2 * TOK : 2 * TOK + TOK // 2]
    far_high[...] = share[2 * TOK + TOK // 2 : 3 * TOK]
    to_last[...] = share[3 * TOK :]


def whole(shape):
    return pl.BlockSpec(shape, lambda *_: (0,) * len(shape))


def columns(rows):
    return pl.BlockSpec((rows, STEP), lambda i, *_: (0, i))


def forward(kind, meta, slots, tokens, tiles):
    rows = (TOK, TOK, TOK // 2, TOK // 2, TOK)
    return pl.pallas_call(
        functools.partial(forward_kernel, kind),
        grid_spec=pltpu.PrefetchScalarGridSpec(
            num_scalar_prefetch=2,
            grid=(FF // STEP,),
            in_specs=[whole(a.shape) for a in (*tokens, *tiles)],
            out_specs=[columns(n) for n in rows] + [whole((ALL, ALL))],
            scratch_shapes=[pltpu.VMEM((ALL, FF), BF16)],
        ),
        out_shape=[jax.ShapeDtypeStruct((n, FF), BF16) for n in rows]
        + [jax.ShapeDtypeStruct((ALL, ALL), BF16)],
        compiler_params=PARAMS,
        cost_estimate=pl.CostEstimate(flops=2 * ALL * ALL * FF, bytes_accessed=12 * 2**20, transcendentals=0),
        name=kind + "_forward",
    )(meta, slots, *tokens, *tiles)


def middle_kernel(g0, g1, g2, u0, u1, u2, cot, hidden, gate_grad, up_grad):
    gate = g0[...].astype(F32) + g1[...].astype(F32) + g2[...].astype(F32)
    up = u0[...].astype(F32) + u1[...].astype(F32) + u2[...].astype(F32)
    upstream = cot[...].astype(F32)
    sigmoid = jax.nn.sigmoid(gate)
    activated = gate * sigmoid
    hidden[...] = (activated * up).astype(BF16)
    gate_grad[...] = (upstream * up * sigmoid * (1.0 + gate * (1.0 - sigmoid))).astype(BF16)
    up_grad[...] = (upstream * activated).astype(BF16)


def middle(gate_terms, up_terms, cotangent):
    return pl.pallas_call(
        middle_kernel,
        grid=(FF // STEP,),
        in_specs=[columns(TOK)] * 7,
        out_specs=[columns(TOK)] * 3,
        out_shape=[jax.ShapeDtypeStruct((TOK, FF), BF16)] * 3,
        compiler_params=PARAMS,
        cost_estimate=pl.CostEstimate(flops=TOK * FF * 20, bytes_accessed=10 * TOK * FF * 2, transcendentals=TOK * FF),
        name="middle",
    )(*gate_terms, *up_terms, cotangent)


def tile_grad_kernel(kind, meta, slots, turned, own, below, above, far_low, far_high, o0, o1, o2a, o2b, o3, grads, slot_of):
    step = pl.program_id(0)

    @pl.when(step == 0)
    def _():
        for ref in (o0, o1, o2a, o2b, o3):
            ref[...] = jnp.zeros(ref.shape, ref.dtype)
        for distance in range(RING):
            base = owner_base(kind, meta, distance)
            for spot in range(ROW_TILES * COL_TILES):
                slot_of[distance * ROW_TILES * COL_TILES + spot] = -1

            def note(index, _, base=base, distance=distance):
                spot = slots[base + index]

                @pl.when(spot >= 0)
                def _():
                    slot_of[distance * ROW_TILES * COL_TILES + spot] = index

                return 0

            lax.fori_loop(0, CAP, note, 0)

    grads[0:TOK] = own[...]
    grads[TOK : 2 * TOK] = above[...]
    grads[2 * TOK : 2 * TOK + TOK // 2] = far_low[...]
    grads[2 * TOK + TOK // 2 : 3 * TOK] = far_high[...]
    grads[3 * TOK :] = below[...]
    for distance in range(RING):
        share = jnp.dot(
            turned[distance * ROWS : (distance + 1) * ROWS], grads[...], preferred_element_type=F32
        ).astype(BF16)
        for r in range(ROW_TILES):
            for b in range(STEP // TILE):
                slot = slot_of[(distance * ROW_TILES + r) * COL_TILES + step * (STEP // TILE) + b]
                tile = share[r * TILE : (r + 1) * TILE, b * TILE : (b + 1) * TILE]
                if distance == 2:

                    @pl.when((slot >= 0) & (slot < HALF))
                    def _(slot=slot, tile=tile):
                        o2a[slot] = tile

                    @pl.when(slot >= HALF)
                    def _(slot=slot, tile=tile):
                        o2b[slot - HALF] = tile

                else:
                    out = (o0, o1, None, o3)[distance]

                    @pl.when(slot >= 0)
                    def _(slot=slot, tile=tile, out=out):
                        out[slot] = tile


def tile_grad(kind, meta, slots, turned, pieces):
    shapes = [(n, TILE, TILE) for n in (CAP, CAP, HALF, HALF, CAP)]
    return pl.pallas_call(
        functools.partial(tile_grad_kernel, kind),
        grid_spec=pltpu.PrefetchScalarGridSpec(
            num_scalar_prefetch=2,
            grid=(FF // STEP,),
            in_specs=[whole((ALL, ALL))] + [columns(a.shape[0]) for a in pieces],
            out_specs=[whole(s) for s in shapes],
            scratch_shapes=[
                pltpu.VMEM((ALL, STEP), BF16),
                pltpu.SMEM((RING * ROW_TILES * COL_TILES,), jnp.int32),
            ],
        ),
        out_shape=[jax.ShapeDtypeStruct(s, BF16) for s in shapes],
        compiler_params=PARAMS,
        cost_estimate=pl.CostEstimate(flops=2 * ALL * ALL * FF, bytes_accessed=9 * 2**20, transcendentals=0),
        name=kind + "_tile_grad",
    )(meta, slots, turned, *pieces)


def input_grad_kernel(kind, meta, slots, *refs):
    tiles, pieces = refs[:5], refs[5:10]
    keep, give, dense, grads = refs[10:]
    y, z, x, c = place_of(meta)
    step = pl.program_id(0)
    by_x = lambda distance: mod(y + distance - x)

    @pl.when(step == 0)
    def _():
        if kind == "gate":
            weight_place, token_place = by_x, lambda distance: mod(distance - 2 * c)
        else:
            weight_place, token_place = (lambda distance: mod(z + distance - 2 * c)), by_x
        fill_weights(kind, meta, slots, tiles, dense, weight_place)
        for ref, distance, first in zip(pieces, (0, 3, 1, 2, 2), (0, 0, 0, 0, TOK // 2)):
            row = pl.multiple_of(token_place(distance) * TOK + first, TILE)
            grads[pl.ds(row, ref.shape[0]), :] = ref[...]

    here = pl.ds(pl.multiple_of(step * 256, 256), 256)
    contract = (((1,), (1,)), ((), ()))
    if kind == "gate":
        share = lax.dot_general(grads[...], dense[here, :], contract, preferred_element_type=F32).astype(BF16)
        keep[0] = share[: ALL // 2]
        give[0] = share[ALL // 2 :]
    else:
        share = lax.dot_general(grads[here, :], dense[...], contract, preferred_element_type=F32).astype(BF16)
        keep[0] = share[:, : ALL // 2]
        give[0] = share[:, ALL // 2 :]


def input_grad(kind, meta, slots, tiles, pieces):
    shape = (RING, 512, 256) if kind == "gate" else (RING, 256, 512)
    block = pl.BlockSpec((1, *shape[1:]), lambda i, *_: (i, 0, 0))
    return pl.pallas_call(
        functools.partial(input_grad_kernel, kind),
        grid_spec=pltpu.PrefetchScalarGridSpec(
            num_scalar_prefetch=2,
            grid=(RING,),
            in_specs=[whole(a.shape) for a in (*tiles, *pieces)],
            out_specs=[block, block],
            scratch_shapes=[pltpu.VMEM((ALL, FF), BF16), pltpu.VMEM((ALL, FF), BF16)],
        ),
        out_shape=[jax.ShapeDtypeStruct(shape, BF16)] * 2,
        compiler_params=PARAMS,
        cost_estimate=pl.CostEstimate(flops=2 * ALL * ALL * FF, bytes_accessed=8 * 2**20, transcendentals=0),
        name=kind + "_input_grad",
    )(meta, slots, *tiles, *pieces)


def exchange_pairs(parity):
    pairs = []
    for z in range(RING):
        for c in range(2):
            to_z = 2 * c + (z + parity) % 2
            pairs.append((z * 2 + c, to_z * 2 + ((z - to_z) % RING) // 2))
    return pairs


TURN = [(y * RING + x, x * RING + y) for y in range(RING) for x in range(RING)]


def per_device(tokens, gate_tiles, up_tiles, gate_slots, up_slots, cotangent):
    y, z, x, c = (lax.axis_index(a) for a in ("y", "z", "x", "core"))
    meta = jnp.stack([y, z, x, c]).astype(jnp.int32)
    gate_slots = gate_slots.reshape(-1)
    up_slots = up_slots.reshape(-1)

    low, high = tokens[:, :256], tokens[:, 256:]
    odd = z % 2 == 1
    even_block = lax.ppermute(jnp.where(odd, high, low), ("z", "core"), exchange_pairs(0))
    odd_block = lax.ppermute(jnp.where(odd, low, high), ("z", "core"), exchange_pairs(1))
    turned = lax.ppermute(tokens, ("y", "x"), TURN)
    gate_pieces = gather_ring(gate_tiles, "y")
    up_pieces = gather_ring(up_tiles, "z")
    gate_tokens = gather_ring(jnp.concatenate([even_block, odd_block], 0), "x")
    up_tokens = gather_ring(turned, "x")
    gate_tokens = gate_tokens + tuple(swap_core(a) for a in gate_tokens)
    up_tokens = up_tokens + tuple(swap_core(a) for a in up_tokens)

    *gate_shares, gate_x = forward("gate", meta, gate_slots, gate_tokens, gate_pieces)
    *up_shares, up_x = forward("up", meta, up_slots, up_tokens, up_pieces)
    gate_terms = scatter_ring(*gate_shares, "z")
    up_terms = scatter_ring(*up_shares, "y")
    hidden, gate_grad, up_grad = middle(gate_terms, up_terms, cotangent)

    gate_grads = gather_ring(gate_grad, "z")
    up_grads = gather_ring(up_grad, "y")
    gate_sums = tile_grad("gate", meta, gate_slots, gate_x.T, gate_grads)
    up_sums = tile_grad("up", meta, up_slots, up_x.T, up_grads)
    gate_out = scatter_ring(*gate_sums, "y")
    up_out = scatter_ring(*up_sums, "z")

    def total(terms):
        return terms[0].astype(F32) + terms[1].astype(F32) + terms[2].astype(F32)

    parts = []
    for kind, slots, tiles, grads in (
        ("gate", gate_slots, gate_pieces, gate_grads),
        ("up", up_slots, up_pieces, up_grads),
    ):
        keep, give = input_grad(kind, meta, slots, tiles, grads)
        both = add(keep, swap_core(give))
        half = both.shape[1] // 2
        parts.append(total(scatter_ring(both[0], both[1], both[2, :half], both[2, half:], both[3], "x")).astype(BF16))
    gate_part, up_part = parts
    even_block, odd_block = (
        lax.ppermute(gate_part[256 * j : 256 * (j + 1)], ("z", "core"), [(b, a) for a, b in exchange_pairs(j)])
        for j in range(2)
    )
    low, high = jnp.where(odd, odd_block, even_block), jnp.where(odd, even_block, odd_block)
    up_part = lax.ppermute(up_part, ("y", "x"), TURN)
    input_sum = add(jnp.concatenate([low, high], 1), up_part)
    return hidden, input_sum, total(gate_out).astype(BF16), total(up_out).astype(BF16)


def solution(mesh):
    grid = Mesh(mesh.devices.reshape(RING, RING, RING, 2), ("y", "z", "x", "core"))
    rows, cols = ("y", "z"), ("x", "core")
    placed = (
        P(rows, cols),
        P(rows, cols, None),
        P(rows, cols, None),
        P(None, cols),
        P(None, cols),
        P(rows, cols),
    )
    return jax.shard_map(
        per_device,
        mesh=grid,
        in_specs=placed,
        out_specs=(P(rows, cols), P(rows, cols), P(rows, cols, None), P(rows, cols, None)),
        check_vma=False,
    )
```

```python
import functools

import jax
import jax.numpy as jnp
from jax import lax
from jax.experimental import pallas as pl
from jax.experimental.pallas import tpu as pltpu
from jax.sharding import Mesh
from jax.sharding import PartitionSpec as P

RING = 4
TILE = 128
CAP = 18
HALF = CAP // 2
ROW_TILES = 2
COL_TILES = 14
TOK = 256
ROWS = ROW_TILES * TILE
FF = COL_TILES * TILE
ALL = RING * 256
STEP = 256
F32 = jnp.float32
BF16 = jnp.bfloat16


def params(mib):
    return pltpu.CompilerParams(vmem_limit_bytes=mib * 2**20)


def shift(value, axis, by):
    return lax.ppermute(value, axis, [(i, (i + by) % RING) for i in range(RING)])


def gather_ring(value, axis):
    half = value.shape[0] // 2
    below = shift(value, axis, 1)
    above = shift(value, axis, -1)
    far_low = shift(below[:half], axis, 1)
    far_high = shift(above[half:], axis, -1)
    return value, below, above, far_low, far_high


def add(a, b):
    return (a.astype(F32) + b.astype(F32)).astype(BF16)


def scatter_ring(own, to_next, far_low, far_high, to_last, axis):
    half = far_low.shape[0]
    low = shift(far_low, axis, 1)
    high = shift(far_high, axis, -1)
    to_next = jnp.concatenate([add(to_next[:half], low), to_next[half:]], 0)
    to_last = jnp.concatenate([to_last[:half], add(to_last[half:], high)], 0)
    return own, shift(to_next, axis, 1), shift(to_last, axis, -1)


def swap_core(value):
    return lax.ppermute(value, "core", [(0, 1), (1, 0)])


def mod(value):
    return lax.rem(value + 2 * RING, RING)


def place_of(meta):
    return meta[0], meta[1], meta[2], meta[3]


def owner_base(kind, meta, distance):
    y, z, _, _ = place_of(meta)
    owner = mod(y + distance) * RING + z if kind == "gate" else y * RING + mod(z + distance)
    return owner * CAP


def tile_copies(kind, meta, slots, pieces, dense, position, sem, act):
    for piece, distance, first, count in zip(pieces, (0, 3, 1, 2, 2), (0, 0, 0, 0, HALF), (CAP, CAP, CAP, HALF, HALF)):
        base = owner_base(kind, meta, distance) + first
        row_base = position(distance) * ROWS

        def put(index, _, piece=piece, base=base, row_base=row_base):
            spot = slots[base + index]

            @pl.when(spot >= 0)
            def _():
                row = pl.multiple_of(row_base + lax.div(spot, COL_TILES) * TILE, TILE)
                col = pl.multiple_of(lax.rem(spot, COL_TILES) * TILE, TILE)
                act(pltpu.make_async_copy(piece.at[index], dense.at[pl.ds(row, TILE), pl.ds(col, TILE)], sem))

            return 0

        lax.fori_loop(0, count, put, 0)


def start(copy):
    copy.start()


def wait(copy):
    copy.wait()


def token_places(kind, meta):
    y, z, x, c = place_of(meta)
    places = []
    pieces = (
        (0, c, 0, 0),
        (1, c, -1, 0),
        (2, c, 1, 0),
        (5, 1 - c, 0, 0),
        (6, 1 - c, -1, 0),
        (7, 1 - c, 1, 0),
    )
    if kind == "gate":
        pieces += ((3, c, 2, 0), (8, 1 - c, 2, 0))
    else:
        pieces += ((4, c, 2, -512), (9, 1 - c, 2, -512))
    for piece, core, distance, first in pieces:
        if kind == "gate":
            col = mod(x + distance - y) * ROWS
            places.append((piece, slice(first, first + 512), 2 * core * TOK, col))
        else:
            row = mod(x + distance - y) * TOK
            for b in range(2):
                begin = first + 512 + 256 * b
                places.append((piece, slice(begin, begin + 256), row, mod(2 * core + b - z) * ROWS))
    return places


def forward_kernel(kind, count, n_tiles, meta, slots, *refs):
    tokens, tiles = refs[:count], refs[count : count + n_tiles]
    *outs, x_out, together, dense, share, token_sem, tile_sem, x_sem, out_sem = refs[count + n_tiles :]
    token_copies = [
        pltpu.make_async_copy(
            tokens[piece].at[rows],
            together.at[
                pl.ds(pl.multiple_of(row, TILE), rows.stop - rows.start),
                pl.ds(pl.multiple_of(col, TILE), ROWS),
            ],
            token_sem,
        )
        for piece, rows, row, col in token_places(kind, meta)
    ]
    for copy in token_copies:
        copy.start()
    dense[...] = jnp.zeros(dense.shape, dense.dtype)
    tile_copies(kind, meta, slots, tiles, dense, lambda distance: distance, tile_sem, start)
    for copy in token_copies:
        copy.wait()
    keep_x = pltpu.make_async_copy(together, x_out, x_sem)
    keep_x.start()
    tile_copies(kind, meta, slots, tiles, dense, lambda distance: distance, tile_sem, wait)
    copies = [keep_x]
    order = ((2, 512, 128), (3, 640, 128), (1, 256, 256), (4, 768, 256), (0, 0, 256))
    for first in (512, 256, 768, 0):
        rows = slice(first, first + TOK)
        for step in range(FF // STEP):
            cols = slice(step * STEP, (step + 1) * STEP)
            share[rows, cols] = jnp.dot(together[rows], dense[:, cols], preferred_element_type=F32).astype(BF16)
        for index, begin, count in order:
            if first <= begin < first + TOK:
                copies.append(pltpu.make_async_copy(share.at[begin : begin + count], outs[index], out_sem.at[index]))
                copies[-1].start()
    for copy in copies:
        copy.wait()


SCALARS = pl.BlockSpec(memory_space=pltpu.SMEM)
STAY = pl.BlockSpec(memory_space=pltpu.HBM)


def forward(kind, meta, slots, tokens, tiles):
    rows = (TOK, TOK, TOK // 2, TOK // 2, TOK)
    dma = pltpu.SemaphoreType.DMA
    return pl.pallas_call(
        functools.partial(forward_kernel, kind, len(tokens), len(tiles)),
        in_specs=[SCALARS] * 2 + [STAY] * len(tokens) + [STAY] * len(tiles),
        out_specs=[STAY] * 6,
        scratch_shapes=[
            pltpu.VMEM((ALL, ALL), BF16),
            pltpu.VMEM((ALL, FF), BF16),
            pltpu.VMEM((ALL, FF), BF16),
            dma,
            dma,
            dma,
            dma((5,)),
        ],
        out_shape=[jax.ShapeDtypeStruct((n, FF), BF16) for n in rows]
        + [jax.ShapeDtypeStruct((ALL, ALL), BF16)],
        compiler_params=params(60),
        cost_estimate=pl.CostEstimate(flops=2 * ALL * ALL * FF, bytes_accessed=12 * 2**20, transcendentals=0),
        name=kind + "_forward",
    )(meta, slots, *tokens, *tiles)


def middle_kernel(g0, g1, g2, u0, u1, u2, cot, hidden, gate_grad, up_grad):
    gate = g0[...].astype(F32) + g1[...].astype(F32) + g2[...].astype(F32)
    up = u0[...].astype(F32) + u1[...].astype(F32) + u2[...].astype(F32)
    upstream = cot[...].astype(F32)
    sigmoid = jax.nn.sigmoid(gate)
    activated = gate * sigmoid
    hidden[...] = (activated * up).astype(BF16)
    gate_grad[...] = (upstream * up * sigmoid * (1.0 + gate * (1.0 - sigmoid))).astype(BF16)
    up_grad[...] = (upstream * activated).astype(BF16)


def middle(gate_terms, up_terms, cotangent):
    block = pl.BlockSpec((32, FF), lambda i: (i, 0))
    return pl.pallas_call(
        middle_kernel,
        grid=(TOK // 32,),
        in_specs=[block] * 7,
        out_specs=[block] * 3,
        out_shape=[jax.ShapeDtypeStruct((TOK, FF), BF16)] * 3,
        compiler_params=params(60),
        cost_estimate=pl.CostEstimate(flops=TOK * FF * 20, bytes_accessed=10 * TOK * FF * 2, transcendentals=TOK * FF),
        name="middle",
    )(*gate_terms, *up_terms, cotangent)


def tile_grad_kernel(kind, meta, slots, turned, *refs):
    pieces, outs = refs[:5], refs[5:10]
    x, grads, dense, zero, x_sem, grad_sem, out_sem = refs[10:]
    x_copy = pltpu.make_async_copy(turned, x, x_sem)
    x_copy.start()
    first_rows = (0, 3 * TOK, TOK, 2 * TOK, 2 * TOK + TOK // 2)
    copies = [
        pltpu.make_async_copy(ref, grads.at[row : row + ref.shape[0]], grad_sem.at[index])
        for index, (ref, row) in enumerate(zip(pieces, first_rows))
    ]
    for copy in copies:
        copy.start()
    zero[...] = jnp.zeros(zero.shape, zero.dtype)
    x_copy.wait()
    for copy in copies:
        copy.wait()
    for step in range(FF // STEP):
        cols = slice(step * STEP, (step + 1) * STEP)
        dense[:, cols] = jnp.dot(x[...], grads[:, cols], preferred_element_type=F32).astype(BF16)
    for act in (start, wait):
        for out, distance, first in zip(outs, (0, 1, 2, 2, 3), (0, 0, 0, HALF, 0)):
            base = owner_base(kind, meta, distance) + first

            def put(index, _, base=base, out=out, distance=distance):
                spot = slots[base + index]

                @pl.when(spot >= 0)
                def _():
                    row = pl.multiple_of(distance * ROWS + lax.div(spot, COL_TILES) * TILE, TILE)
                    col = pl.multiple_of(lax.rem(spot, COL_TILES) * TILE, TILE)
                    act(pltpu.make_async_copy(dense.at[pl.ds(row, TILE), pl.ds(col, TILE)], out.at[index], out_sem))

                @pl.when(spot < 0)
                def _():
                    act(pltpu.make_async_copy(zero, out.at[index], out_sem))

                return 0

            lax.fori_loop(0, out.shape[0], put, 0)


def tile_grad(kind, meta, slots, turned, pieces):
    shapes = [(n, TILE, TILE) for n in (CAP, CAP, HALF, HALF, CAP)]
    dma = pltpu.SemaphoreType.DMA
    return pl.pallas_call(
        functools.partial(tile_grad_kernel, kind),
        in_specs=[SCALARS] * 2 + [STAY] * 6,
        out_specs=[STAY] * 5,
        scratch_shapes=[
            pltpu.VMEM((ALL, ALL), BF16),
            pltpu.VMEM((ALL, FF), BF16),
            pltpu.VMEM((ALL, FF), BF16),
            pltpu.VMEM((TILE, TILE), BF16),
            dma,
            dma((5,)),
            dma,
        ],
        out_shape=[jax.ShapeDtypeStruct(s, BF16) for s in shapes],
        compiler_params=params(60),
        cost_estimate=pl.CostEstimate(flops=2 * ALL * ALL * FF, bytes_accessed=9 * 2**20, transcendentals=0),
        name=kind + "_tile_grad",
    )(meta, slots, turned, *pieces)


def input_grad_kernel(distances, refs_per_kind, aliased, meta, gate_slots, up_slots, *refs):
    n = refs_per_kind
    gate_tiles, gate_pieces, up_tiles, up_pieces = refs[0:5], refs[5 : 5 + n], refs[5 + n : 10 + n], refs[10 + n : 10 + 2 * n]
    keep, give, dense, grads, share, tile_sem, grad_sem, out_sem = refs[10 + 2 * n + aliased :]
    y, z, x, c = place_of(meta)

    def by_x(distance):
        return mod(y + distance - x)

    def by_feature(distance):
        return mod(z + distance - 2 * c)

    kinds = (
        ("gate", gate_slots, gate_tiles, gate_pieces, by_x),
        ("up", up_slots, up_tiles, up_pieces, by_feature),
    )
    grad_copies = []
    for index, (kind, slots, tiles, pieces, weight_place) in enumerate(kinds):
        grad_copies.append([])
        row = 0
        for ref in pieces:
            grad_copies[-1].append(
                pltpu.make_async_copy(ref, grads.at[index, row : row + ref.shape[0]], grad_sem.at[index])
            )
            grad_copies[-1][-1].start()
            row += ref.shape[0]
        dense[index] = jnp.zeros(dense.shape[1:], dense.dtype)
        tile_copies(kind, meta, slots, tiles, dense.at[index], weight_place, tile_sem.at[index], start)
    contract = (((1,), (1,)), ((), ()))
    outs = []
    for index, (kind, slots, tiles, pieces, weight_place) in enumerate(kinds):
        tile_copies(kind, meta, slots, tiles, dense.at[index], weight_place, tile_sem.at[index], wait)
        for copy in grad_copies[index]:
            copy.wait()
        for block in range(RING):
            weights = dense[index, block * ROWS : (block + 1) * ROWS]
            share[index, block] = lax.dot_general(grads[index], weights, contract, preferred_element_type=F32).astype(BF16)
        for number, distance in enumerate(distances):
            rows = slice(number * TOK, (number + 1) * TOK)
            if kind == "gate":
                spot = mod(distance - 2 * c)
                row = pl.multiple_of(lax.rem(spot, 2) * TOK, TOK)
                copies = [
                    pltpu.make_async_copy(share.at[0, :, rows], out.at[:, pl.ds(row, TOK)], out_sem.at[0]) for out in (keep, give)
                ]
                pl.when(spot < 2)(copies[0].start)
                pl.when(spot >= 2)(copies[1].start)
                outs.append(copies[0])
            else:
                to = by_x(distance)
                for block in range(RING):
                    first = 512 + 256 * (block % 2)
                    out = (keep, give)[block // 2]
                    copy = pltpu.make_async_copy(share.at[1, block, rows], out.at[to, first : first + 256], out_sem.at[1])
                    copy.start()
                    outs.append(copy)
    for copy in outs:
        copy.wait()


def input_grad(distances, meta, gate_slots, up_slots, gate_tiles, gate_grads, up_tiles, up_grads, sofar=()):
    dma = pltpu.SemaphoreType.DMA
    tokens = TOK * len(distances)
    shape = jax.ShapeDtypeStruct((RING, ALL, 256), BF16)
    operands = (meta, gate_slots, up_slots, *gate_tiles, *gate_grads, *up_tiles, *up_grads)
    count = len(operands)
    return pl.pallas_call(
        functools.partial(input_grad_kernel, distances, len(gate_grads), len(sofar)),
        in_specs=[SCALARS] * 3 + [STAY] * (count - 3 + len(sofar)),
        out_specs=[STAY] * 2,
        scratch_shapes=[
            pltpu.VMEM((2, ALL, FF), BF16),
            pltpu.VMEM((2, tokens, FF), BF16),
            pltpu.VMEM((2, RING, tokens, 256), BF16),
            dma((2,)),
            dma((2,)),
            dma((2,)),
        ],
        out_shape=[shape] * 2,
        input_output_aliases={count + i: i for i in range(len(sofar))},
        compiler_params=params(60),
        cost_estimate=pl.CostEstimate(
            flops=4 * ALL * tokens * FF, bytes_accessed=10 * 2**20 + tokens * FF * 4, transcendentals=0
        ),
        name="input_grad_" + "_".join(map(str, distances)),
    )(*operands, *sofar)


def exchange_pairs(parity):
    pairs = []
    for z in range(RING):
        for c in range(2):
            to_z = 2 * c + (z + parity) % 2
            pairs.append((z * 2 + c, to_z * 2 + ((z - to_z) % RING) // 2))
    return pairs


TURN = [(y * RING + x, x * RING + y) for y in range(RING) for x in range(RING)]


def per_device(tokens, gate_tiles, up_tiles, gate_slots, up_slots, cotangent):
    y, z, x, c = (lax.axis_index(a) for a in ("y", "z", "x", "core"))
    meta = jnp.stack([y, z, x, c]).astype(jnp.int32)
    gate_slots = gate_slots.reshape(-1)
    up_slots = up_slots.reshape(-1)

    low, high = tokens[:, :256], tokens[:, 256:]
    odd = z % 2 == 1
    gate_below, gate_above, even_block, odd_block, turned = lax.optimization_barrier((
        shift(gate_tiles, "y", 1),
        shift(gate_tiles, "y", -1),
        lax.ppermute(jnp.where(odd, high, low), ("z", "core"), exchange_pairs(0)),
        lax.ppermute(jnp.where(odd, low, high), ("z", "core"), exchange_pairs(1)),
        lax.ppermute(tokens, ("y", "x"), TURN),
    ))
    held = jnp.concatenate([even_block, odd_block, turned[:, :256], turned[:, 256:]], 0)
    held, up_tiles, gate_below, gate_above = lax.optimization_barrier((held, up_tiles, gate_below, gate_above))
    below, above, up_below, up_above, gate_low, gate_high = lax.optimization_barrier((
        shift(held, "x", 1),
        shift(held, "x", -1),
        shift(up_tiles, "z", 1),
        shift(up_tiles, "z", -1),
        shift(gate_below[:HALF], "y", 1),
        shift(gate_above[HALF:], "y", -1),
    ))
    far_gate, far_up, held_swap, below_swap, above_swap, up_low, up_high = lax.optimization_barrier((
        shift(below[:512], "x", 1),
        shift(above[512:], "x", -1),
        swap_core(held),
        swap_core(below),
        swap_core(above),
        shift(up_below[:HALF], "z", 1),
        shift(up_above[HALF:], "z", -1),
    ))
    all_tokens = (held, below, above, far_gate, far_up, held_swap, below_swap, above_swap, swap_core(far_gate), swap_core(far_up))
    gate_pieces = (gate_tiles, gate_below, gate_above, gate_low, gate_high)
    up_pieces = (up_tiles, up_below, up_above, up_low, up_high)

    *gate_shares, gate_x = forward("gate", meta, gate_slots, all_tokens, gate_pieces)
    *up_shares, up_x = forward("up", meta, up_slots, all_tokens, up_pieces)
    gate_terms = scatter_ring(*gate_shares, "z")
    up_terms = scatter_ring(*up_shares, "y")
    gate_turned, up_turned, cotangent = lax.optimization_barrier((gate_x.T, up_x.T, cotangent))
    hidden, gate_grad, up_grad = middle(gate_terms, up_terms, cotangent)

    gate_grads = gather_ring(gate_grad, "z")
    up_grads = gather_ring(up_grad, "y")
    gate_sums = tile_grad("gate", meta, gate_slots, gate_turned, gate_grads)
    up_sums = tile_grad("up", meta, up_slots, up_turned, up_grads)
    gate_out = scatter_ring(*gate_sums, "y")
    up_out = scatter_ring(*up_sums, "z")

    def total(terms):
        return terms[0].astype(F32) + terms[1].astype(F32) + terms[2].astype(F32)

    near = input_grad((0, 3, 1), meta, gate_slots, up_slots, gate_pieces, gate_grads[:3], up_pieces, up_grads[:3])
    keep, give = input_grad((2,), meta, gate_slots, up_slots, gate_pieces, gate_grads[3:], up_pieces, up_grads[3:], near)
    both = add(keep, swap_core(give))
    part = total(scatter_ring(both[0], both[1], both[2, :512], both[2, 512:], both[3], "x")).astype(BF16)
    gate_part = part[:512]
    up_part = jnp.concatenate([part[512:768], part[768:]], 1)
    even_block, odd_block = (
        lax.ppermute(gate_part[256 * j : 256 * (j + 1)], ("z", "core"), [(b, a) for a, b in exchange_pairs(j)])
        for j in range(2)
    )
    low, high = jnp.where(odd, odd_block, even_block), jnp.where(odd, even_block, odd_block)
    up_part = lax.ppermute(up_part, ("y", "x"), TURN)
    input_sum = add(jnp.concatenate([low, high], 1), up_part)
    return hidden, input_sum, total(gate_out).astype(BF16), total(up_out).astype(BF16)


def solution(mesh):
    grid = Mesh(mesh.devices.reshape(RING, RING, RING, 2), ("y", "z", "x", "core"))
    rows, cols = ("y", "z"), ("x", "core")
    placed = (
        P(rows, cols),
        P(rows, cols, None),
        P(rows, cols, None),
        P(None, cols),
        P(None, cols),
        P(rows, cols),
    )
    return jax.shard_map(
        per_device,
        mesh=grid,
        in_specs=placed,
        out_specs=(P(rows, cols), P(rows, cols), P(rows, cols, None), P(rows, cols, None)),
        check_vma=False,
    )
```
